32 devices in a mesh: beam: 2 (over y), chan: 4 (over z), tile: 2 (over x), pol: 2 (over core).
Axes of the slice: x: 2, y: 2, z: 4, core: 2. Of those that a mesh axis runs over, the one named last changes fastest.
Arguments:
- voltages: bfloat16 [8, 32, 100000], P(('beam', 'tile', 'pol'), 'chan'), parts along dimension 0, may hold values from -6 to 6
- flagged: int32 [4, 32], P(('tile', 'pol'), 'chan'), may hold values 0 or 1
- channel_table: int32 [4], replicated, may hold values from 0 to 3, each once
Outputs:
- visibilities: float32 [2, 8, 128, 128], P(None, ('beam', 'chan'), ('tile', 'pol')), parts along dimension 1
The draws below stay inside these ranges and needn't reach their ends.
There are 2 independent parts, one for each index of `beam`. The reference program is written for one: setup_inputs(seed, part) draws one part's arguments, and reference() takes and returns one part's arrays. A program takes and returns all parts, laid end to end along the dimension named above; an argument that names none is the same for every part. Nothing has to cross between parts.
Inputs may be any that keep to these rules, and one draw needn't show every extreme that they name: `flagged`: 1 marks an input whose spectra are zeroed. `channel_table`: a permutation of the 4 channel blocks.
All inputs are finite; a program needn't handle non-finite values. No bound on the sum of `flagged` on one device may be relied on, other than what follows from the above.
Results may differ from the reference program's by a relative error of at most 0.0012.
Values may be sent and summed in bfloat16 or wider, within the bound.
A program may use at most 64 MiB of HBM per device.

```python
import math
import jax
import jax.numpy as jnp
import numpy as np
from jax import lax

TAPS = 4
FRAMES = 2
NFFT = 20000
NCH = 10000
CHB = 2500
BLK = 32
GROUPS = 4
INPUTS = 128
SAMPLES = 100000
N_CHAN = 4


def with_ends(values, rng, least, top_value):
    spot = [jax.random.randint(jax.random.fold_in(rng, axis), (), 0, length) for axis, length in enumerate(values.shape)]
    longest = values.shape.index(max(values.shape))
    beside = spot[:longest] + [(spot[longest] + 1) % values.shape[longest]] + spot[longest + 1:]
    return values.at[tuple(spot)].set(least).at[tuple(beside)].set(top_value)


def level_of(stream_key, shape, pieces, least, largest):
    def one(dim, shards_of):
        draws = jax.random.uniform(jax.random.fold_in(jax.random.fold_in(stream_key, 6), dim), (shards_of,), jnp.float32, least / len(pieces), largest / len(pieces))
        return jnp.repeat(jnp.exp(draws), shape[dim] // shards_of).reshape((-1,) + (1,) * (len(shape) - dim - 1))

    factor_of = one(*pieces[0])
    for cut in pieces[1:]:
        factor_of = factor_of * one(*cut)
    return factor_of


def noise(own_key, extent, scale, most, split=(), kind=jnp.bfloat16):
    drawn = jax.random.normal(own_key, extent, jnp.float32) * scale
    if len(split) > 0:
        drawn = level_of(own_key, extent, split, -0.22, 0.18) * drawn
    return jnp.clip(drawn, min=-most, max=most).astype(kind)


def setup_inputs(seed: int = 0, part: int = 0) -> dict:
    streams_of = jax.random.split(jax.random.key(seed), 4)
    own_keys = jax.random.split(jax.random.fold_in(streams_of[3], part), 4)
    voltages = noise(own_keys[0], (GROUPS, BLK, SAMPLES), 1.0, 6.0, ((0, 4), (1, 4)))
    flagged = with_ends((jax.random.randint(streams_of[1], (GROUPS, BLK), 0, 8) < 1).astype(jnp.int32), jax.random.fold_in(streams_of[1], 1), 0, 1)
    channel_table = jax.random.permutation(streams_of[2], N_CHAN).astype(jnp.int32)
    return {"voltages": voltages, "flagged": flagged, "channel_table": channel_table}


def window_table(tap_count, frame_len):
    position = np.arange(tap_count * frame_len) * 1.0
    centre = (position - tap_count * frame_len / 2.0 + 0.5) / frame_len
    shaped = np.sin(np.pi * centre) / (np.pi * centre)
    prototype = shaped * (0.5 - 0.5 * np.cos(2.0 * np.pi * (position + 0.5) / (tap_count * frame_len)))
    prototype = prototype / np.sqrt(np.sum(prototype * prototype) / frame_len)
    return prototype.reshape(tap_count, frame_len)

def spectra_of(group_samples, group_flags):
    filt = jnp.asarray(window_table(TAPS, NFFT), jnp.float32)
    frames_all = group_samples.astype(jnp.float32).reshape(BLK, FRAMES + TAPS - 1, NFFT)
    filtered = jnp.zeros((BLK, FRAMES, NFFT), jnp.float32)
    for tap_index in range(TAPS):
        filtered = filtered + filt[tap_index] * frames_all[:, tap_index:tap_index + FRAMES]
    spectrum = jnp.fft.fft(filtered, axis=-1)[..., :NCH] / math.sqrt(NFFT)
    kept = (1 - group_flags).astype(jnp.float32)[:, None, None]
    stacked = jnp.stack([jnp.real(spectrum) * kept, jnp.imag(spectrum) * kept], axis=1)
    return stacked.astype(jnp.bfloat16)

def reference(voltages, flagged, channel_table):
    spectra = lax.map(lambda pair: spectra_of(pair[0], pair[1]), (voltages, flagged))
    spectra = spectra.reshape(INPUTS, 2, FRAMES, NCH)
    scale = 1.0 / math.sqrt(FRAMES * CHB)
    half_len = FRAMES * CHB

    def band(block_id):
        first = (block_id * CHB).astype(jnp.int32)
        picked = lax.dynamic_slice_in_dim(spectra, first, CHB, axis=3)
        left_rows = picked.reshape(INPUTS, 2 * half_len)
        swapped = jnp.concatenate([left_rows[:, half_len:], -left_rows[:, :half_len]], axis=1)
        real_part = jnp.dot(left_rows, left_rows.T, preferred_element_type=jnp.float32) * scale
        imag_part = jnp.dot(swapped, left_rows.T, preferred_element_type=jnp.float32) * scale
        return jnp.stack([real_part, imag_part], axis=0)
    result = lax.map(band, channel_table)
    return jnp.moveaxis(result, 0, 1)
```

```python
import functools
import math

import jax
import jax.numpy as jnp
import numpy as np
from jax import lax
from jax.experimental import pallas as pl
from jax.experimental.pallas import tpu as pltpu
from jax.sharding import PartitionSpec as P

N_OUTER = 160
N_INNER = 125
TAPS = 4
FRAMES = 2


def window_table(tap_count, frame_len):
    position = np.arange(tap_count * frame_len) * 1.0
    centre = (position - tap_count * frame_len / 2.0 + 0.5) / frame_len
    shaped = np.sin(np.pi * centre) / (np.pi * centre)
    prototype = shaped * (
        0.5 - 0.5 * np.cos(2.0 * np.pi * (position + 0.5) / (tap_count * frame_len))
    )
    prototype = prototype / np.sqrt(np.sum(prototype * prototype) / frame_len)
    return prototype.reshape(tap_count, frame_len)


def make_spectra(samples_in, flags_in, channel_table, n_chan):
    in_dev = samples_in.shape[0]
    frame_len = N_OUTER * N_INNER
    half_len = N_OUTER // 2
    filt = jnp.asarray(window_table(TAPS, frame_len), jnp.float32)
    frames_all = samples_in.astype(jnp.float32).reshape(in_dev, FRAMES + TAPS - 1, frame_len)
    filtered = jnp.zeros((in_dev, FRAMES, frame_len), jnp.float32)
    for tap_index in range(TAPS):
        filtered = filtered + filt[tap_index] * frames_all[:, tap_index : tap_index + FRAMES]
    filtered = filtered.reshape(in_dev, FRAMES, N_INNER, N_OUTER)
    inner_idx = jnp.arange(N_INNER, dtype=jnp.int32)
    inner_ang = (
        2.0
        * math.pi
        / N_INNER
        * (inner_idx[:, None] * inner_idx[None, :] % N_INNER).astype(jnp.float32)
    )
    inner_mat = jnp.concatenate([jnp.cos(inner_ang), -jnp.sin(inner_ang)], axis=0)
    section_one = jnp.einsum("kn,vsnm->vskm", inner_mat, filtered, precision=lax.Precision.HIGH)
    real_one = section_one[:, :, :N_INNER]
    imag_one = section_one[:, :, N_INNER:]
    outer_idx = jnp.arange(N_OUTER, dtype=jnp.int32)
    twist_ang = (
        2.0
        * math.pi
        / frame_len
        * (inner_idx[:, None] * outer_idx[None, :] % frame_len).astype(jnp.float32)
    )
    twist_cos = jnp.cos(twist_ang)
    twist_sin = jnp.sin(twist_ang)
    real_two = real_one * twist_cos + imag_one * twist_sin
    imag_two = imag_one * twist_cos - real_one * twist_sin
    joined = jnp.concatenate([real_two, imag_two], axis=3)
    block_width = half_len // n_chan
    out_pos = jnp.arange(half_len, dtype=jnp.int32)
    owner = out_pos // block_width
    onehot = owner[:, None] == jnp.arange(n_chan, dtype=jnp.int32)[None, :]
    chosen = jnp.sum(jnp.where(onehot, channel_table[None, :], 0), axis=1)
    outer_k = chosen * block_width + out_pos % block_width
    outer_ang = (
        2.0
        * math.pi
        / N_OUTER
        * (outer_k[:, None] * outer_idx[None, :] % N_OUTER).astype(jnp.float32)
    )
    outer_cos = jnp.cos(outer_ang)
    outer_sin = jnp.sin(outer_ang)
    real_rows = jnp.concatenate([outer_cos, outer_sin], axis=1)
    imag_rows = jnp.concatenate([-outer_sin, outer_cos], axis=1)
    outer_mat = jnp.stack([real_rows, imag_rows], axis=0)
    spectrum = jnp.einsum("vskn,rjn->vrsjk", joined, outer_mat, precision=lax.Precision.HIGH)
    spectrum = spectrum.reshape(in_dev, 2, FRAMES, half_len * N_INNER)
    kept_mask = (1 - flags_in).astype(jnp.float32)
    spectrum = spectrum * (kept_mask[:, None, None, None] / math.sqrt(frame_len))
    return spectrum.astype(jnp.bfloat16)


def correlate(left_rows, panel_cols, scale):
    return (
        jnp.einsum("rik,jk->rij", left_rows, panel_cols, preferred_element_type=jnp.float32) * scale
    )


def on_device(voltages, flagged, channel_table):
    n_chan = lax.axis_size("chan")
    spectra = make_spectra(voltages[0], flagged[0], channel_table, n_chan)
    turned = lax.all_to_all(spectra, "chan", split_axis=3, concat_axis=0, tiled=True)
    group_len = turned.shape[0]
    chb_len = turned.shape[3]
    half_k = FRAMES * chb_len
    scale = 1.0 / math.sqrt(FRAMES * chb_len)
    band_rows = turned.reshape(group_len, 2 * half_k)
    swapped = jnp.concatenate([band_rows[:, half_k:], -band_rows[:, :half_k]], axis=1)
    left_rows = jnp.stack([band_rows, swapped], axis=0)
    vis_local = correlate(
        left_rows, lax.all_gather(band_rows, ("tile", "pol"), axis=0, tiled=True), scale
    )
    return vis_local[:, None]


MESH = pl.DeviceIdType.MESH
LANES = 128
A_LEN = 625
A_PAD = 640
K0_HALF = 313
K0_PAD = 320
R_ALL = 16
IN_DEV = 8
HALF_IN = 4
ROWS = 16
WIDE = FRAMES * K0_PAD


def split_bf16(table):
    high = table.astype(jnp.bfloat16)
    low = (table - high.astype(np.float64)).astype(jnp.bfloat16)
    return high, low


def tables(n_groups, n_chan):
    frame_len = N_OUTER * N_INNER
    window = window_table(TAPS, frame_len).reshape(-1).astype(np.float32).astype(np.float64)
    shift = frame_len // LANES
    win = np.zeros((FRAMES, A_PAD * LANES))
    win[0, : window.size] = window
    offset = frame_len - shift * LANES
    win[1, offset : offset + window.size] = window
    win = win.reshape(FRAMES, A_PAD, LANES)

    k0 = np.arange(K0_HALF)
    a = np.arange(A_LEN + 1)
    ang = 2.0 * np.pi / A_LEN * ((4 * k0[:, None] * a[None, :]) % A_LEN)
    dft = np.zeros((2, K0_PAD, A_PAD))
    dft[0, :K0_HALF, : A_LEN + 1] = np.cos(ang)
    dft[1, :K0_HALF, : A_LEN + 1] = -np.sin(ang)
    dft = dft.reshape(2 * K0_PAD, A_PAD)

    b = np.arange(LANES)
    twist = np.zeros((FRAMES, 2, K0_PAD, LANES))
    for s in range(FRAMES):
        first = s * shift * LANES
        ang = 2.0 * np.pi / frame_len * ((k0[:, None] * (b[None, :] + first)) % frame_len)
        twist[s, 0, :K0_HALF] = np.cos(ang)
        twist[s, 1, :K0_HALF] = np.sin(ang)
    twist = twist / math.sqrt(frame_len)

    r = np.arange(R_ALL)
    ang = 2.0 * np.pi / 32 * ((r[:, None] * b[None, :]) % 32)
    mir = 2.0 * np.pi / 32 * (((31 - r)[:, None] * b[None, :]) % 32)
    outer = np.zeros((R_ALL, 4, 2, LANES))
    outer[:, 0, 0], outer[:, 0, 1] = np.cos(ang), np.sin(ang)
    outer[:, 1, 0], outer[:, 1, 1] = -np.sin(ang), np.cos(ang)
    outer[:, 2, 0], outer[:, 2, 1] = np.cos(mir), np.sin(mir)
    outer[:, 3, 0], outer[:, 3, 1] = np.sin(mir), -np.cos(mir)
    outer = outer.reshape(n_chan, n_groups * 4, 2 * LANES)
    outer = np.stack(split_bf16(outer), axis=1)

    n_src = n_groups * n_chan
    perm = np.zeros((4, n_src * IN_DEV, 2, n_src, 4, HALF_IN))
    for src in range(n_src):
        for h in range(2):
            for i in range(HALF_IN):
                for q in range(4):
                    perm[q, src * IN_DEV + h * HALF_IN + i, h, src, q, i] = 1.0
    size = 4 * n_src * IN_DEV
    perm = perm.reshape(size, size).astype(jnp.bfloat16)
    dft_high, dft_low = split_bf16(dft)
    return win.astype(np.float32), dft_high, dft_low, twist.astype(np.float32), outer, perm


def kernel(
    n_chan, n_tile, n_pol, volt_ref, flag_ref, table_ref, win_ref, dh_ref, dl_ref, twist_ref,
    outer_ref, perm_ref, out_ref, flat, u_high, u_low, zt, turned, send, recv, left, vpart, vrecv,
    send_sem, recv_sem, vsend_sem, vrecv_sem,
):
    n_groups = n_tile * n_pol
    c, t, p = lax.axis_index("chan"), lax.axis_index("tile"), lax.axis_index("pol")
    g = t * n_pol + p
    src = g * n_chan + c

    def peers():
        found = []
        for dc in range(n_chan - 1, -1, -1):
            for dt in range(n_tile - 1, -1, -1):
                for dp in range(n_pol - 1, -1, -1):
                    if dc or dt or dp:
                        found.append(((c + dc) % n_chan, (t + dt) % n_tile, (p + dp) % n_pol))
        return found

    def where(peer):
        return {"chan": peer[0], "tile": peer[1], "pol": peer[2]}

    everyone = peers()
    barrier = pltpu.get_barrier_semaphore()
    for peer in everyone:
        pl.semaphore_signal(barrier, inc=1, device_id=where(peer), device_id_type=MESH)

    tiles_full = volt_ref.shape[2] // LANES
    rest = volt_ref.shape[2] - tiles_full * LANES
    flat[pl.ds(tiles_full * IN_DEV, flat.shape[0] - tiles_full * IN_DEV), :] = jnp.zeros(
        (flat.shape[0] - tiles_full * IN_DEV, LANES), jnp.float32
    )
    if rest:
        flat[pl.ds(tiles_full * IN_DEV, IN_DEV), pl.ds(0, rest)] = volt_ref[
            0, :, pl.ds(tiles_full * LANES, rest)
        ].astype(jnp.float32)

    step = 11

    def spread(chunk, carry):
        for j in range(step):
            tile = chunk * step + j
            lane = pl.multiple_of(tile * LANES, LANES)
            row = pl.multiple_of(tile * IN_DEV, IN_DEV)
            flat[pl.ds(row, IN_DEV), :] = volt_ref[0, :, pl.ds(lane, LANES)].astype(jnp.float32)
        return carry

    lax.fori_loop(0, tiles_full // step, spread, 0)

    outer_rows = jnp.concatenate(
        [outer_ref[table_ref[b], part] for part in range(2) for b in range(n_chan)], axis=0
    )
    shift = N_OUTER * N_INNER // LANES
    n_rows = R_ALL * 4
    row_id = lax.broadcasted_iota(jnp.int32, (n_rows, WIDE), 0)
    lane_id = lax.broadcasted_iota(jnp.int32, (n_rows, WIDE), 1)
    twice = ((row_id % 4) >= 2) & ((lane_id == 0) | (lane_id == K0_PAD))
    once = jnp.where(twice, 0.0, 1.0)

    for h in range(2):
        for i in range(HALF_IN):
            for s in range(FRAMES):
                first = s * shift * IN_DEV + h * HALF_IN + i
                col = (i * FRAMES + s) * LANES
                u = flat[pl.ds(first, A_PAD, stride=IN_DEV), :] * win_ref[s]
                high = u.astype(jnp.bfloat16)
                u_high[:, col : col + LANES] = high
                u_low[:, col : col + LANES] = (u - high.astype(jnp.float32)).astype(jnp.bfloat16)
        for i in range(HALF_IN):
            for s in range(FRAMES):
                col = (i * FRAMES + s) * LANES
                if s == 0:
                    wide = pl.ds(i * FRAMES * LANES, FRAMES * LANES)
                    uh, ul = u_high[:, wide], u_low[:, wide]
                    y = (
                        jnp.dot(dh_ref[...], uh, preferred_element_type=jnp.float32)
                        + jnp.dot(dl_ref[...], uh, preferred_element_type=jnp.float32)
                        + jnp.dot(dh_ref[...], ul, preferred_element_type=jnp.float32)
                    )
                yr = y[:K0_PAD, s * LANES : (s + 1) * LANES]
                yi = y[K0_PAD:, s * LANES : (s + 1) * LANES]
                co, si = twist_ref[s, 0], twist_ref[s, 1]
                zt[i % 2, pl.ds(s * K0_PAD, K0_PAD), 0:LANES] = (yr * co + yi * si).astype(jnp.bfloat16)
                zt[i % 2, pl.ds(s * K0_PAD, K0_PAD), LANES : 2 * LANES] = (yi * co - yr * si).astype(
                    jnp.bfloat16
                )
            x = lax.dot_general(
                outer_rows, zt[i % 2], (((1,), (1,)), ((), ())), preferred_element_type=jnp.float32
            )
            keep = (1 - flag_ref[0, h * HALF_IN + i]).astype(jnp.float32)
            x = (x[:n_rows] + x[n_rows:]) * (once * keep)
            for l in range(WIDE // LANES):
                turned[l, pl.ds(i, n_rows, stride=HALF_IN), :] = x[:, l * LANES : (l + 1) * LANES]
        for l in range(WIDE // LANES):
            send[h, :, :, pl.ds(l * LANES, LANES)] = (
                turned[l].astype(jnp.bfloat16).reshape(R_ALL, ROWS, LANES)
            )
        if h == 0:
            pl.semaphore_wait(barrier, len(everyone))
        for d, peer in enumerate(everyone):
            slot = peer[0] * n_groups + peer[1] * n_pol + peer[2]
            pltpu.make_async_remote_copy(
                src_ref=send.at[h, slot],
                dst_ref=recv.at[h, src],
                send_sem=send_sem.at[h, d],
                recv_sem=recv_sem.at[h, d],
                device_id=where(peer),
                device_id_type=MESH,
            ).start()
        recv[h, src] = send[h, c * n_groups + g]

    for h in range(2):
        for d, peer in enumerate(everyone):
            slot = peer[0] * n_groups + peer[1] * n_pol + peer[2]
            pltpu.make_async_remote_copy(
                src_ref=send.at[h, slot],
                dst_ref=recv.at[h, src],
                send_sem=send_sem.at[h, d],
                recv_sem=recv_sem.at[h, d],
                device_id=where(peer),
                device_id_type=MESH,
            ).wait()

    n_in = n_groups * n_chan * IN_DEV
    got = recv[...].reshape(4 * n_in, WIDE)
    for q in range(4):
        part = jnp.dot(
            perm_ref[pl.ds(q * n_in, n_in), :], got, preferred_element_type=jnp.float32
        ).astype(jnp.bfloat16)
        left[0:n_in, pl.ds(q * WIDE, WIDE)] = part
        if q % 2 == 0:
            left[n_in : 2 * n_in, pl.ds((q + 1) * WIDE, WIDE)] = -part
        else:
            left[n_in : 2 * n_in, pl.ds((q - 1) * WIDE, WIDE)] = part
    vis = lax.dot_general(
        left[...], left[0:n_in, :], (((1,), (1,)), ((), ())), preferred_element_type=jnp.float32
    )
    vis = vis * (1.0 / math.sqrt(FRAMES * n_groups * A_LEN))
    rows = n_in // n_groups
    for k in range(n_groups):
        vpart[k, 0:rows] = vis[k * rows : (k + 1) * rows]
        vpart[k, rows : 2 * rows] = vis[n_in + k * rows : n_in + (k + 1) * rows]

    moves = []
    for dt in range(n_tile - 1, -1, -1):
        for dp in range(n_pol - 1, -1, -1):
            if dt or dp:
                pt, pp = (t + dt) % n_tile, (p + dp) % n_pol
                d = len(moves)
                move = pltpu.make_async_remote_copy(
                    src_ref=vpart.at[pt * n_pol + pp],
                    dst_ref=vrecv.at[d],
                    send_sem=vsend_sem.at[d],
                    recv_sem=vrecv_sem.at[d],
                    device_id={"tile": pt, "pol": pp},
                    device_id_type=MESH,
                )
                move.start()
                moves.append(move)
    total = vpart[g]
    for d, move in enumerate(moves):
        move.wait()
        total = total + vrecv[d]
    out_ref[0, 0] = total[:rows]
    out_ref[1, 0] = total[rows:]


def on_device_kernel(n_chan, n_tile, n_pol, voltages, flagged, channel_table):
    n_groups = n_tile * n_pol
    n_src = n_groups * n_chan
    n_in = n_src * IN_DEV
    consts = [jnp.asarray(x) for x in tables(n_groups, n_chan)]
    vmem = pl.BlockSpec(memory_space=pltpu.VMEM)
    smem = pl.BlockSpec(memory_space=pltpu.SMEM)
    rows = n_in // n_groups
    tiles = -(-voltages.shape[2] // LANES)
    tall = max(tiles, N_OUTER * N_INNER // LANES + A_PAD)
    return pl.pallas_call(
        functools.partial(kernel, n_chan, n_tile, n_pol),
        out_shape=jax.ShapeDtypeStruct((2, 1, rows, n_in), jnp.float32),
        in_specs=[vmem, smem, smem] + [vmem] * 6,
        out_specs=vmem,
        scratch_shapes=[
            pltpu.VMEM((tall * IN_DEV, LANES), jnp.float32),
            pltpu.VMEM((A_PAD, HALF_IN * FRAMES * LANES), jnp.bfloat16),
            pltpu.VMEM((A_PAD, HALF_IN * FRAMES * LANES), jnp.bfloat16),
            pltpu.VMEM((2, WIDE, 2 * LANES), jnp.bfloat16),
            pltpu.VMEM((WIDE // LANES, R_ALL * ROWS, LANES), jnp.float32),
            pltpu.VMEM((2, R_ALL, ROWS, WIDE), jnp.bfloat16),
            pltpu.VMEM((2, n_src, ROWS, WIDE), jnp.bfloat16),
            pltpu.VMEM((2 * n_in, 4 * WIDE), jnp.bfloat16),
            pltpu.VMEM((n_groups, 2 * rows, n_in), jnp.float32),
            pltpu.VMEM((n_groups - 1, 2 * rows, n_in), jnp.float32),
            pltpu.SemaphoreType.DMA((2, n_src - 1)),
            pltpu.SemaphoreType.DMA((2, n_src - 1)),
            pltpu.SemaphoreType.DMA((n_groups - 1,)),
            pltpu.SemaphoreType.DMA((n_groups - 1,)),
        ],
        compiler_params=pltpu.CompilerParams(
            collective_id=0, has_side_effects=True, vmem_limit_bytes=48 * 1024 * 1024
        ),
    )(voltages, flagged, channel_table, *consts)


def solution(mesh):
    n_chan, n_tile, n_pol = mesh.shape["chan"], mesh.shape["tile"], mesh.shape["pol"]
    body = on_device
    if n_chan * n_tile * n_pol == R_ALL:
        body = functools.partial(on_device_kernel, n_chan, n_tile, n_pol)
    in_specs = (P(("beam", "tile", "pol"), "chan", None), P(("tile", "pol"), "chan"), P())
    out_specs = P(None, ("beam", "chan"), ("tile", "pol"), None)
    return jax.shard_map(
        body, mesh=mesh, in_specs=in_specs, out_specs=out_specs, check_vma=False
    )
```

```python
import functools
import math

import jax
import jax.numpy as jnp
import numpy as np
from jax import lax
from jax.experimental import pallas as pl
from jax.experimental.pallas import tpu as pltpu
from jax.sharding import PartitionSpec as P

N_OUTER = 160
N_INNER = 125
TAPS = 4
FRAMES = 2


def window_table(tap_count, frame_len):
    position = np.arange(tap_count * frame_len) * 1.0
    centre = (position - tap_count * frame_len / 2.0 + 0.5) / frame_len
    shaped = np.sin(np.pi * centre) / (np.pi * centre)
    prototype = shaped * (
        0.5 - 0.5 * np.cos(2.0 * np.pi * (position + 0.5) / (tap_count * frame_len))
    )
    prototype = prototype / np.sqrt(np.sum(prototype * prototype) / frame_len)
    return prototype.reshape(tap_count, frame_len)


def make_spectra(samples_in, flags_in, channel_table, n_chan):
    in_dev = samples_in.shape[0]
    frame_len = N_OUTER * N_INNER
    half_len = N_OUTER // 2
    filt = jnp.asarray(window_table(TAPS, frame_len), jnp.float32)
    frames_all = samples_in.astype(jnp.float32).reshape(in_dev, FRAMES + TAPS - 1, frame_len)
    filtered = jnp.zeros((in_dev, FRAMES, frame_len), jnp.float32)
    for tap_index in range(TAPS):
        filtered = filtered + filt[tap_index] * frames_all[:, tap_index : tap_index + FRAMES]
    filtered = filtered.reshape(in_dev, FRAMES, N_INNER, N_OUTER)
    inner_idx = jnp.arange(N_INNER, dtype=jnp.int32)
    inner_ang = (
        2.0
        * math.pi
        / N_INNER
        * (inner_idx[:, None] * inner_idx[None, :] % N_INNER).astype(jnp.float32)
    )
    inner_mat = jnp.concatenate([jnp.cos(inner_ang), -jnp.sin(inner_ang)], axis=0)
    section_one = jnp.einsum("kn,vsnm->vskm", inner_mat, filtered, precision=lax.Precision.HIGH)
    real_one = section_one[:, :, :N_INNER]
    imag_one = section_one[:, :, N_INNER:]
    outer_idx = jnp.arange(N_OUTER, dtype=jnp.int32)
    twist_ang = (
        2.0
        * math.pi
        / frame_len
        * (inner_idx[:, None] * outer_idx[None, :] % frame_len).astype(jnp.float32)
    )
    twist_cos = jnp.cos(twist_ang)
    twist_sin = jnp.sin(twist_ang)
    real_two = real_one * twist_cos + imag_one * twist_sin
    imag_two = imag_one * twist_cos - real_one * twist_sin
    joined = jnp.concatenate([real_two, imag_two], axis=3)
    block_width = half_len // n_chan
    out_pos = jnp.arange(half_len, dtype=jnp.int32)
    owner = out_pos // block_width
    onehot = owner[:, None] == jnp.arange(n_chan, dtype=jnp.int32)[None, :]
    chosen = jnp.sum(jnp.where(onehot, channel_table[None, :], 0), axis=1)
    outer_k = chosen * block_width + out_pos % block_width
    outer_ang = (
        2.0
        * math.pi
        / N_OUTER
        * (outer_k[:, None] * outer_idx[None, :] % N_OUTER).astype(jnp.float32)
    )
    outer_cos = jnp.cos(outer_ang)
    outer_sin = jnp.sin(outer_ang)
    real_rows = jnp.concatenate([outer_cos, outer_sin], axis=1)
    imag_rows = jnp.concatenate([-outer_sin, outer_cos], axis=1)
    outer_mat = jnp.stack([real_rows, imag_rows], axis=0)
    spectrum = jnp.einsum("vskn,rjn->vrsjk", joined, outer_mat, precision=lax.Precision.HIGH)
    spectrum = spectrum.reshape(in_dev, 2, FRAMES, half_len * N_INNER)
    kept_mask = (1 - flags_in).astype(jnp.float32)
    spectrum = spectrum * (kept_mask[:, None, None, None] / math.sqrt(frame_len))
    return spectrum.astype(jnp.bfloat16)


def correlate(left_rows, panel_cols, scale):
    return (
        jnp.einsum("rik,jk->rij", left_rows, panel_cols, preferred_element_type=jnp.float32) * scale
    )


def on_device(voltages, flagged, channel_table):
    n_chan = lax.axis_size("chan")
    spectra = make_spectra(voltages[0], flagged[0], channel_table, n_chan)
    turned = lax.all_to_all(spectra, "chan", split_axis=3, concat_axis=0, tiled=True)
    group_len = turned.shape[0]
    chb_len = turned.shape[3]
    half_k = FRAMES * chb_len
    scale = 1.0 / math.sqrt(FRAMES * chb_len)
    band_rows = turned.reshape(group_len, 2 * half_k)
    swapped = jnp.concatenate([band_rows[:, half_k:], -band_rows[:, :half_k]], axis=1)
    left_rows = jnp.stack([band_rows, swapped], axis=0)
    vis_local = correlate(
        left_rows, lax.all_gather(band_rows, ("tile", "pol"), axis=0, tiled=True), scale
    )
    return vis_local[:, None]


MESH = pl.DeviceIdType.MESH
LANES = 128
A_LEN = 625
A_PAD = 640
K0_HALF = 313
K0_PAD = 320
R_ALL = 16
IN_DEV = 8
HALF_IN = 4
ROWS = 16
WIDE = FRAMES * K0_PAD


def split_bf16(table):
    high = table.astype(jnp.bfloat16)
    low = (table - high.astype(np.float64)).astype(jnp.bfloat16)
    return high, low


def tables(n_groups, n_chan):
    frame_len = N_OUTER * N_INNER
    window = window_table(TAPS, frame_len).reshape(-1).astype(np.float32).astype(np.float64)
    shift = frame_len // LANES
    win = np.zeros((FRAMES, A_PAD * LANES))
    win[0, : window.size] = window
    offset = frame_len - shift * LANES
    win[1, offset : offset + window.size] = window
    win = win.reshape(FRAMES, A_PAD, LANES)

    k0 = np.arange(K0_HALF)
    a = np.arange(A_LEN + 1)
    ang = 2.0 * np.pi / A_LEN * ((4 * k0[:, None] * a[None, :]) % A_LEN)
    dft = np.zeros((2, K0_PAD, A_PAD))
    dft[0, :K0_HALF, : A_LEN + 1] = np.cos(ang)
    dft[1, :K0_HALF, : A_LEN + 1] = -np.sin(ang)
    dft = dft.reshape(2 * K0_PAD, A_PAD)

    b = np.arange(LANES)
    twist = np.zeros((FRAMES, 2, K0_PAD, LANES))
    for s in range(FRAMES):
        first = s * shift * LANES
        ang = 2.0 * np.pi / frame_len * ((k0[:, None] * (b[None, :] + first)) % frame_len)
        twist[s, 0, :K0_HALF] = np.cos(ang)
        twist[s, 1, :K0_HALF] = np.sin(ang)
    twist = twist / math.sqrt(frame_len)

    r = np.arange(R_ALL)
    ang = 2.0 * np.pi / 32 * ((r[:, None] * b[None, :]) % 32)
    mir = 2.0 * np.pi / 32 * (((31 - r)[:, None] * b[None, :]) % 32)
    outer = np.zeros((R_ALL, 4, 2, LANES))
    outer[:, 0, 0], outer[:, 0, 1] = np.cos(ang), np.sin(ang)
    outer[:, 1, 0], outer[:, 1, 1] = -np.sin(ang), np.cos(ang)
    outer[:, 2, 0], outer[:, 2, 1] = np.cos(mir), np.sin(mir)
    outer[:, 3, 0], outer[:, 3, 1] = np.sin(mir), -np.cos(mir)
    outer = outer.reshape(n_chan, n_groups * 4, 2 * LANES)
    outer = np.stack(split_bf16(outer), axis=1)

    n_src = n_groups * n_chan
    perm = np.zeros((4, n_src * IN_DEV, 2, n_src, 4, HALF_IN))
    for src in range(n_src):
        for h in range(2):
            for i in range(HALF_IN):
                for q in range(4):
                    perm[q, src * IN_DEV + h * HALF_IN + i, h, src, q, i] = 1.0
    size = 4 * n_src * IN_DEV
    perm = perm.reshape(size, size).astype(jnp.bfloat16)
    dft_high, dft_low = split_bf16(dft)
    return win.astype(np.float32), dft_high, dft_low, twist.astype(np.float32), outer, perm


def kernel(
    n_chan, n_tile, n_pol, volt_hbm, flag_hbm, table_hbm, win_hbm, dh_hbm, dl_hbm, twist_hbm,
    outer_hbm, perm_hbm, out_ref, volt_ref, flag_ref, table_ref, win_ref, dh_ref, dl_ref, twist_ref,
    outer_ref, perm_ref, flat, u_high, u_low, zt, turned, send, recv, left, vpart, vrecv,
    load_sem, send_sem, recv_sem, vsend_sem, vrecv_sem,
):
    loads = [
        pltpu.make_async_copy(source, target, load_sem.at[n])
        for n, (source, target) in enumerate(
            [
                (volt_hbm, volt_ref), (win_hbm, win_ref), (dh_hbm, dh_ref), (dl_hbm, dl_ref),
                (twist_hbm, twist_ref), (outer_hbm, outer_ref), (flag_hbm, flag_ref),
                (table_hbm, table_ref), (perm_hbm, perm_ref),
            ]
        )
    ]
    for load in loads:
        load.start()
    n_groups = n_tile * n_pol
    c, t, p = lax.axis_index("chan"), lax.axis_index("tile"), lax.axis_index("pol")
    g = t * n_pol + p
    src = g * n_chan + c

    def peers():
        found = []
        for dc in range(n_chan - 1, -1, -1):
            for dt in range(n_tile - 1, -1, -1):
                for dp in range(n_pol - 1, -1, -1):
                    if dc or dt or dp:
                        found.append(((c + dc) % n_chan, (t + dt) % n_tile, (p + dp) % n_pol))
        return found

    def where(peer):
        return {"chan": peer[0], "tile": peer[1], "pol": peer[2]}

    everyone = peers()
    barrier = pltpu.get_barrier_semaphore()
    for peer in everyone:
        pl.semaphore_signal(barrier, inc=1, device_id=where(peer), device_id_type=MESH)

    tiles_full = volt_ref.shape[2] // LANES
    rest = volt_ref.shape[2] - tiles_full * LANES
    flat[pl.ds(tiles_full * IN_DEV, flat.shape[0] - tiles_full * IN_DEV), :] = jnp.zeros(
        (flat.shape[0] - tiles_full * IN_DEV, LANES), jnp.float32
    )
    step = 71
    loads[0].wait()
    if rest:
        flat[pl.ds(tiles_full * IN_DEV, IN_DEV), pl.ds(0, rest)] = volt_ref[
            0, :, pl.ds(tiles_full * LANES, rest)
        ].astype(jnp.float32)

    def spread(chunk, carry):
        for j in range(step):
            tile = chunk * step + j
            lane = pl.multiple_of(tile * LANES, LANES)
            row = pl.multiple_of(tile * IN_DEV, IN_DEV)
            flat[pl.ds(row, IN_DEV), :] = volt_ref[0, :, pl.ds(lane, LANES)].astype(jnp.float32)
        return carry

    lax.fori_loop(0, tiles_full // step, spread, 0)

    for load in loads[1:8]:
        load.wait()
    outer_rows = jnp.concatenate(
        [outer_ref[table_ref[b], part] for part in range(2) for b in range(n_chan)], axis=0
    )
    shift = N_OUTER * N_INNER // LANES
    n_rows = R_ALL * 4
    row_id = lax.broadcasted_iota(jnp.int32, (n_rows, WIDE), 0)
    lane_id = lax.broadcasted_iota(jnp.int32, (n_rows, WIDE), 1)
    twice = ((row_id % 4) >= 2) & ((lane_id == 0) | (lane_id == K0_PAD))
    once = jnp.where(twice, 0.0, 1.0)

    for h in range(2):
        for i in range(HALF_IN):
            for s in range(FRAMES):
                first = s * shift * IN_DEV + h * HALF_IN + i
                col = (i * FRAMES + s) * LANES
                u = flat[pl.ds(first, A_PAD, stride=IN_DEV), :] * win_ref[s]
                high = u.astype(jnp.bfloat16)
                u_high[:, col : col + LANES] = high
                u_low[:, col : col + LANES] = (u - high.astype(jnp.float32)).astype(jnp.bfloat16)
        for i in range(HALF_IN):
            for s in range(FRAMES):
                col = (i * FRAMES + s) * LANES
                if s == 0:
                    wide = pl.ds(i * FRAMES * LANES, FRAMES * LANES)
                    uh, ul = u_high[:, wide], u_low[:, wide]
                    y = (
                        jnp.dot(dh_ref[...], uh, preferred_element_type=jnp.float32)
                        + jnp.dot(dl_ref[...], uh, preferred_element_type=jnp.float32)
                        + jnp.dot(dh_ref[...], ul, preferred_element_type=jnp.float32)
                    )
                yr = y[:K0_PAD, s * LANES : (s + 1) * LANES]
                yi = y[K0_PAD:, s * LANES : (s + 1) * LANES]
                co, si = twist_ref[s, 0], twist_ref[s, 1]
                zt[i % 2, pl.ds(s * K0_PAD, K0_PAD), 0:LANES] = (yr * co + yi * si).astype(jnp.bfloat16)
                zt[i % 2, pl.ds(s * K0_PAD, K0_PAD), LANES : 2 * LANES] = (yi * co - yr * si).astype(
                    jnp.bfloat16
                )
            x = lax.dot_general(
                outer_rows, zt[i % 2], (((1,), (1,)), ((), ())), preferred_element_type=jnp.float32
            )
            keep = (1 - flag_ref[0, h * HALF_IN + i]).astype(jnp.float32)
            x = (x[:n_rows] + x[n_rows:]) * (once * keep)
            for l in range(WIDE // LANES):
                turned[l, pl.ds(i, n_rows, stride=HALF_IN), :] = x[:, l * LANES : (l + 1) * LANES]
        for l in range(WIDE // LANES):
            send[h, :, :, pl.ds(l * LANES, LANES)] = (
                turned[l].astype(jnp.bfloat16).reshape(R_ALL, ROWS, LANES)
            )
        if h == 0:
            pl.semaphore_wait(barrier, len(everyone))
        for d, peer in enumerate(everyone):
            slot = peer[0] * n_groups + peer[1] * n_pol + peer[2]
            pltpu.make_async_remote_copy(
                src_ref=send.at[h, slot],
                dst_ref=recv.at[h, src],
                send_sem=send_sem.at[h, d],
                recv_sem=recv_sem.at[h, d],
                device_id=where(peer),
                device_id_type=MESH,
            ).start()
        recv[h, src] = send[h, c * n_groups + g]

    for h in range(2):
        for d, peer in enumerate(everyone):
            slot = peer[0] * n_groups + peer[1] * n_pol + peer[2]
            pltpu.make_async_remote_copy(
                src_ref=send.at[h, slot],
                dst_ref=recv.at[h, src],
                send_sem=send_sem.at[h, d],
                recv_sem=recv_sem.at[h, d],
                device_id=where(peer),
                device_id_type=MESH,
            ).wait()

    n_in = n_groups * n_chan * IN_DEV
    loads[8].wait()
    got = recv[...].reshape(4 * n_in, WIDE)
    for q in range(4):
        part = jnp.dot(
            perm_ref[pl.ds(q * n_in, n_in), :], got, preferred_element_type=jnp.float32
        ).astype(jnp.bfloat16)
        left[0:n_in, pl.ds(q * WIDE, WIDE)] = part
        if q % 2 == 0:
            left[n_in : 2 * n_in, pl.ds((q + 1) * WIDE, WIDE)] = -part
        else:
            left[n_in : 2 * n_in, pl.ds((q - 1) * WIDE, WIDE)] = part
    vis = lax.dot_general(
        left[...], left[0:n_in, :], (((1,), (1,)), ((), ())), preferred_element_type=jnp.float32
    )
    vis = vis * (1.0 / math.sqrt(FRAMES * n_groups * A_LEN))
    rows = n_in // n_groups
    for k in range(n_groups):
        vpart[k, 0:rows] = vis[k * rows : (k + 1) * rows]
        vpart[k, rows : 2 * rows] = vis[n_in + k * rows : n_in + (k + 1) * rows]

    moves = []
    for dt in range(n_tile - 1, -1, -1):
        for dp in range(n_pol - 1, -1, -1):
            if dt or dp:
                pt, pp = (t + dt) % n_tile, (p + dp) % n_pol
                d = len(moves)
                move = pltpu.make_async_remote_copy(
                    src_ref=vpart.at[pt * n_pol + pp],
                    dst_ref=vrecv.at[d],
                    send_sem=vsend_sem.at[d],
                    recv_sem=vrecv_sem.at[d],
                    device_id={"tile": pt, "pol": pp},
                    device_id_type=MESH,
                )
                move.start()
                moves.append(move)
    total = vpart[g]
    for d, move in enumerate(moves):
        move.wait()
        total = total + vrecv[d]
    out_ref[0, 0] = total[:rows]
    out_ref[1, 0] = total[rows:]


def on_device_kernel(n_chan, n_tile, n_pol, voltages, flagged, channel_table):
    n_groups = n_tile * n_pol
    n_src = n_groups * n_chan
    n_in = n_src * IN_DEV
    consts = [jnp.asarray(x) for x in tables(n_groups, n_chan)]
    vmem = pl.BlockSpec(memory_space=pltpu.VMEM)
    operands = [voltages, flagged, channel_table, *consts]
    spaces = [pltpu.VMEM, pltpu.SMEM, pltpu.SMEM] + [pltpu.VMEM] * len(consts)
    rows = n_in // n_groups
    tiles = -(-voltages.shape[2] // LANES)
    tall = max(tiles, N_OUTER * N_INNER // LANES + A_PAD)
    return pl.pallas_call(
        functools.partial(kernel, n_chan, n_tile, n_pol),
        out_shape=jax.ShapeDtypeStruct((2, 1, rows, n_in), jnp.float32),
        in_specs=[pl.BlockSpec(memory_space=pl.ANY)] * len(operands),
        out_specs=vmem,
        scratch_shapes=[space(x.shape, x.dtype) for space, x in zip(spaces, operands)]
        + [
            pltpu.VMEM((tall * IN_DEV, LANES), jnp.float32),
            pltpu.VMEM((A_PAD, HALF_IN * FRAMES * LANES), jnp.bfloat16),
            pltpu.VMEM((A_PAD, HALF_IN * FRAMES * LANES), jnp.bfloat16),
            pltpu.VMEM((2, WIDE, 2 * LANES), jnp.bfloat16),
            pltpu.VMEM((WIDE // LANES, R_ALL * ROWS, LANES), jnp.float32),
            pltpu.VMEM((2, R_ALL, ROWS, WIDE), jnp.bfloat16),
            pltpu.VMEM((2, n_src, ROWS, WIDE), jnp.bfloat16),
            pltpu.VMEM((2 * n_in, 4 * WIDE), jnp.bfloat16),
            pltpu.VMEM((n_groups, 2 * rows, n_in), jnp.float32),
            pltpu.VMEM((n_groups - 1, 2 * rows, n_in), jnp.float32),
            pltpu.SemaphoreType.DMA((len(operands),)),
            pltpu.SemaphoreType.DMA((2, n_src - 1)),
            pltpu.SemaphoreType.DMA((2, n_src - 1)),
            pltpu.SemaphoreType.DMA((n_groups - 1,)),
            pltpu.SemaphoreType.DMA((n_groups - 1,)),
        ],
        compiler_params=pltpu.CompilerParams(
            collective_id=0, has_side_effects=True, vmem_limit_bytes=60 * 1024 * 1024
        ),
    )(*operands)


def solution(mesh):
    n_chan, n_tile, n_pol = mesh.shape["chan"], mesh.shape["tile"], mesh.shape["pol"]
    body = on_device
    if n_chan * n_tile * n_pol == R_ALL:
        body = functools.partial(on_device_kernel, n_chan, n_tile, n_pol)
    in_specs = (P(("beam", "tile", "pol"), "chan", None), P(("tile", "pol"), "chan"), P())
    out_specs = P(None, ("beam", "chan"), ("tile", "pol"), None)
    return jax.shard_map(
        body, mesh=mesh, in_specs=in_specs, out_specs=out_specs, check_vma=False
    )
```

```python
import functools
import math

import jax
import jax.numpy as jnp
import numpy as np
from jax import lax
from jax.experimental import pallas as pl
from jax.experimental.pallas import tpu as pltpu
from jax.sharding import PartitionSpec as P

N_OUTER = 160
N_INNER = 125
TAPS = 4
FRAMES = 2


def window_table(tap_count, frame_len):
    position = np.arange(tap_count * frame_len) * 1.0
    centre = (position - tap_count * frame_len / 2.0 + 0.5) / frame_len
    shaped = np.sin(np.pi * centre) / (np.pi * centre)
    prototype = shaped * (
        0.5 - 0.5 * np.cos(2.0 * np.pi * (position + 0.5) / (tap_count * frame_len))
    )
    prototype = prototype / np.sqrt(np.sum(prototype * prototype) / frame_len)
    return prototype.reshape(tap_count, frame_len)


def make_spectra(samples_in, flags_in, channel_table, n_chan):
    in_dev = samples_in.shape[0]
    frame_len = N_OUTER * N_INNER
    half_len = N_OUTER // 2
    filt = jnp.asarray(window_table(TAPS, frame_len), jnp.float32)
    frames_all = samples_in.astype(jnp.float32).reshape(in_dev, FRAMES + TAPS - 1, frame_len)
    filtered = jnp.zeros((in_dev, FRAMES, frame_len), jnp.float32)
    for tap_index in range(TAPS):
        filtered = filtered + filt[tap_index] * frames_all[:, tap_index : tap_index + FRAMES]
    filtered = filtered.reshape(in_dev, FRAMES, N_INNER, N_OUTER)
    inner_idx = jnp.arange(N_INNER, dtype=jnp.int32)
    inner_ang = (
        2.0
        * math.pi
        / N_INNER
        * (inner_idx[:, None] * inner_idx[None, :] % N_INNER).astype(jnp.float32)
    )
    inner_mat = jnp.concatenate([jnp.cos(inner_ang), -jnp.sin(inner_ang)], axis=0)
    section_one = jnp.einsum("kn,vsnm->vskm", inner_mat, filtered, precision=lax.Precision.HIGH)
    real_one = section_one[:, :, :N_INNER]
    imag_one = section_one[:, :, N_INNER:]
    outer_idx = jnp.arange(N_OUTER, dtype=jnp.int32)
    twist_ang = (
        2.0
        * math.pi
        / frame_len
        * (inner_idx[:, None] * outer_idx[None, :] % frame_len).astype(jnp.float32)
    )
    twist_cos = jnp.cos(twist_ang)
    twist_sin = jnp.sin(twist_ang)
    real_two = real_one * twist_cos + imag_one * twist_sin
    imag_two = imag_one * twist_cos - real_one * twist_sin
    joined = jnp.concatenate([real_two, imag_two], axis=3)
    block_width = half_len // n_chan
    out_pos = jnp.arange(half_len, dtype=jnp.int32)
    owner = out_pos // block_width
    onehot = owner[:, None] == jnp.arange(n_chan, dtype=jnp.int32)[None, :]
    chosen = jnp.sum(jnp.where(onehot, channel_table[None, :], 0), axis=1)
    outer_k = chosen * block_width + out_pos % block_width
    outer_ang = (
        2.0
        * math.pi
        / N_OUTER
        * (outer_k[:, None] * outer_idx[None, :] % N_OUTER).astype(jnp.float32)
    )
    outer_cos = jnp.cos(outer_ang)
    outer_sin = jnp.sin(outer_ang)
    real_rows = jnp.concatenate([outer_cos, outer_sin], axis=1)
    imag_rows = jnp.concatenate([-outer_sin, outer_cos], axis=1)
    outer_mat = jnp.stack([real_rows, imag_rows], axis=0)
    spectrum = jnp.einsum("vskn,rjn->vrsjk", joined, outer_mat, precision=lax.Precision.HIGH)
    spectrum = spectrum.reshape(in_dev, 2, FRAMES, half_len * N_INNER)
    kept_mask = (1 - flags_in).astype(jnp.float32)
    spectrum = spectrum * (kept_mask[:, None, None, None] / math.sqrt(frame_len))
    return spectrum.astype(jnp.bfloat16)


def correlate(left_rows, panel_cols, scale):
    return (
        jnp.einsum("rik,jk->rij", left_rows, panel_cols, preferred_element_type=jnp.float32) * scale
    )


def on_device(voltages, flagged, channel_table):
    n_chan = lax.axis_size("chan")
    spectra = make_spectra(voltages[0], flagged[0], channel_table, n_chan)
    turned = lax.all_to_all(spectra, "chan", split_axis=3, concat_axis=0, tiled=True)
    group_len = turned.shape[0]
    chb_len = turned.shape[3]
    half_k = FRAMES * chb_len
    scale = 1.0 / math.sqrt(FRAMES * chb_len)
    band_rows = turned.reshape(group_len, 2 * half_k)
    swapped = jnp.concatenate([band_rows[:, half_k:], -band_rows[:, :half_k]], axis=1)
    left_rows = jnp.stack([band_rows, swapped], axis=0)
    vis_local = correlate(
        left_rows, lax.all_gather(band_rows, ("tile", "pol"), axis=0, tiled=True), scale
    )
    return vis_local[:, None]


MESH = pl.DeviceIdType.MESH
LANES = 128
A_LEN = 625
A_PAD = 640
K0_HALF = 313
K0_PAD = 320
R_ALL = 16
IN_DEV = 8
HALF_IN = 4
ROWS = 16
WIDE = FRAMES * K0_PAD


def split_bf16(table):
    high = table.astype(jnp.bfloat16)
    low = (table - high.astype(np.float64)).astype(jnp.bfloat16)
    return high, low


def tables(n_groups, n_chan):
    frame_len = N_OUTER * N_INNER
    window = window_table(TAPS, frame_len).reshape(-1).astype(np.float32).astype(np.float64)
    shift = frame_len // LANES
    win = np.zeros((FRAMES, A_PAD * LANES))
    win[0, : window.size] = window
    offset = frame_len - shift * LANES
    win[1, offset : offset + window.size] = window
    win = win.reshape(FRAMES, A_PAD, LANES)

    k0 = np.arange(K0_HALF)
    a = np.arange(A_LEN + 1)
    ang = 2.0 * np.pi / A_LEN * ((4 * k0[:, None] * a[None, :]) % A_LEN)
    dft = np.zeros((2, K0_PAD, A_PAD))
    dft[0, :K0_HALF, : A_LEN + 1] = np.cos(ang)
    dft[1, :K0_HALF, : A_LEN + 1] = -np.sin(ang)
    dft = dft.reshape(2 * K0_PAD, A_PAD)

    b = np.arange(LANES)
    twist = np.zeros((FRAMES, 2, K0_PAD, LANES))
    for s in range(FRAMES):
        first = s * shift * LANES
        ang = 2.0 * np.pi / frame_len * ((k0[:, None] * (b[None, :] + first)) % frame_len)
        twist[s, 0, :K0_HALF] = np.cos(ang)
        twist[s, 1, :K0_HALF] = np.sin(ang)
    twist = twist / math.sqrt(frame_len)

    r = np.arange(R_ALL)
    ang = 2.0 * np.pi / 32 * ((r[:, None] * b[None, :]) % 32)
    mir = 2.0 * np.pi / 32 * (((31 - r)[:, None] * b[None, :]) % 32)
    outer = np.zeros((R_ALL, 4, 2, LANES))
    outer[:, 0, 0], outer[:, 0, 1] = np.cos(ang), np.sin(ang)
    outer[:, 1, 0], outer[:, 1, 1] = -np.sin(ang), np.cos(ang)
    outer[:, 2, 0], outer[:, 2, 1] = np.cos(mir), np.sin(mir)
    outer[:, 3, 0], outer[:, 3, 1] = np.sin(mir), -np.cos(mir)
    outer = outer.reshape(n_chan, n_groups * 4, 2 * LANES)
    outer = np.stack(split_bf16(outer), axis=1)

    n_src = n_groups * n_chan
    perm = np.zeros((4, n_src * IN_DEV, 2, n_src, 4, HALF_IN))
    for src in range(n_src):
        for h in range(2):
            for i in range(HALF_IN):
                for q in range(4):
                    perm[q, src * IN_DEV + h * HALF_IN + i, h, src, q, i] = 1.0
    size = 4 * n_src * IN_DEV
    perm = perm.reshape(size, size).astype(jnp.bfloat16)
    return win.astype(np.float32), dft.astype(jnp.bfloat16), twist.astype(np.float32), outer, perm


def kernel(
    n_chan, n_tile, n_pol, volt_hbm, flag_hbm, table_hbm, win_hbm, dh_hbm, twist_hbm,
    outer_hbm, perm_hbm, out_ref, volt_ref, flag_ref, table_ref, win_ref, dh_ref, twist_ref,
    outer_ref, perm_ref, flat, u_all, zt, turned, send, recv, left, vpart, vrecv,
    load_sem, send_sem, recv_sem, vsend_sem, vrecv_sem,
):
    loads = [
        pltpu.make_async_copy(source, target, load_sem.at[n])
        for n, (source, target) in enumerate(
            [
                (volt_hbm, volt_ref), (win_hbm, win_ref), (dh_hbm, dh_ref),
                (twist_hbm, twist_ref), (outer_hbm, outer_ref), (flag_hbm, flag_ref),
                (table_hbm, table_ref), (perm_hbm, perm_ref),
            ]
        )
    ]
    for load in loads:
        load.start()
    n_groups = n_tile * n_pol
    c, t, p = lax.axis_index("chan"), lax.axis_index("tile"), lax.axis_index("pol")
    g = t * n_pol + p
    src = g * n_chan + c

    def peers():
        found = []
        for dc in sorted(range(n_chan), key=lambda dc: (dc == 0, abs(2 * dc - n_chan))):
            for dt in range(n_tile - 1, -1, -1):
                for dp in range(n_pol - 1, -1, -1):
                    if dc or dt or dp:
                        found.append(((c + dc) % n_chan, (t + dt) % n_tile, (p + dp) % n_pol))
        return found

    def where(peer):
        return {"chan": peer[0], "tile": peer[1], "pol": peer[2]}

    everyone = peers()
    barrier = pltpu.get_barrier_semaphore()
    for peer in everyone:
        pl.semaphore_signal(barrier, inc=1, device_id=where(peer), device_id_type=MESH)

    tiles_full = volt_ref.shape[2] // LANES
    rest = volt_ref.shape[2] - tiles_full * LANES
    flat[pl.ds(tiles_full * IN_DEV, flat.shape[0] - tiles_full * IN_DEV), :] = jnp.zeros(
        (flat.shape[0] - tiles_full * IN_DEV, LANES), jnp.float32
    )
    step = 71
    loads[0].wait()
    if rest:
        flat[pl.ds(tiles_full * IN_DEV, IN_DEV), pl.ds(0, rest)] = volt_ref[
            0, :, pl.ds(tiles_full * LANES, rest)
        ].astype(jnp.float32)

    def spread(chunk, carry):
        for j in range(step):
            tile = chunk * step + j
            lane = pl.multiple_of(tile * LANES, LANES)
            row = pl.multiple_of(tile * IN_DEV, IN_DEV)
            flat[pl.ds(row, IN_DEV), :] = volt_ref[0, :, pl.ds(lane, LANES)].astype(jnp.float32)
        return carry

    lax.fori_loop(0, tiles_full // step, spread, 0)

    for load in loads[1:7]:
        load.wait()
    outer_rows = jnp.concatenate(
        [outer_ref[table_ref[b], part] for part in range(2) for b in range(n_chan)], axis=0
    )
    shift = N_OUTER * N_INNER // LANES
    n_rows = R_ALL * 4
    row_id = lax.broadcasted_iota(jnp.int32, (n_rows, WIDE), 0)
    lane_id = lax.broadcasted_iota(jnp.int32, (n_rows, WIDE), 1)
    twice = ((row_id % 4) >= 2) & ((lane_id == 0) | (lane_id == K0_PAD))
    once = jnp.where(twice, 0.0, 1.0)

    for h in range(2):
        for i in range(HALF_IN):
            for s in range(FRAMES):
                first = s * shift * IN_DEV + h * HALF_IN + i
                col = (i * FRAMES + s) * LANES
                u = flat[pl.ds(first, A_PAD, stride=IN_DEV), :] * win_ref[s]
                u_all[h, :, col : col + LANES] = u.astype(jnp.bfloat16)
        for i in range(HALF_IN):
            for s in range(FRAMES):
                col = (i * FRAMES + s) * LANES
                if s == 0:
                    wide = pl.ds(i * FRAMES * LANES, FRAMES * LANES)
                    y = jnp.dot(dh_ref[...], u_all[h, :, wide], preferred_element_type=jnp.float32)
                yr = y[:K0_PAD, s * LANES : (s + 1) * LANES]
                yi = y[K0_PAD:, s * LANES : (s + 1) * LANES]
                co, si = twist_ref[s, 0], twist_ref[s, 1]
                zt[i % 2, pl.ds(s * K0_PAD, K0_PAD), 0:LANES] = (yr * co + yi * si).astype(jnp.bfloat16)
                zt[i % 2, pl.ds(s * K0_PAD, K0_PAD), LANES : 2 * LANES] = (yi * co - yr * si).astype(
                    jnp.bfloat16
                )
            x = lax.dot_general(
                outer_rows, zt[i % 2], (((1,), (1,)), ((), ())), preferred_element_type=jnp.float32
            )
            keep = (1 - flag_ref[0, h * HALF_IN + i]).astype(jnp.float32)
            x = (x[:n_rows] + x[n_rows:]) * (once * keep)
            for l in range(WIDE // LANES):
                turned[l, pl.ds(i, n_rows, stride=HALF_IN), :] = x[:, l * LANES : (l + 1) * LANES]
        for l in range(WIDE // LANES):
            send[h, :, :, pl.ds(l * LANES, LANES)] = (
                turned[l].astype(jnp.bfloat16).reshape(R_ALL, ROWS, LANES)
            )
        if h == 0:
            pl.semaphore_wait(barrier, len(everyone))
        for d, peer in enumerate(everyone):
            slot = peer[0] * n_groups + peer[1] * n_pol + peer[2]
            pltpu.make_async_remote_copy(
                src_ref=send.at[h, slot],
                dst_ref=recv.at[h, src],
                send_sem=send_sem.at[h, d],
                recv_sem=recv_sem.at[h, d],
                device_id=where(peer),
                device_id_type=MESH,
            ).start()
        recv[h, src] = send[h, c * n_groups + g]

    loads[7].wait()
    n_in = n_groups * n_chan * IN_DEV
    half_rows = n_groups * n_chan * ROWS
    for h in range(2):
        for d, peer in enumerate(everyone):
            slot = peer[0] * n_groups + peer[1] * n_pol + peer[2]
            pltpu.make_async_remote_copy(
                src_ref=send.at[h, slot],
                dst_ref=recv.at[h, src],
                send_sem=send_sem.at[h, d],
                recv_sem=recv_sem.at[h, d],
                device_id=where(peer),
                device_id_type=MESH,
            ).wait()
        got = recv[h].reshape(half_rows, WIDE)
        for q in range(4):
            part = jnp.dot(
                perm_ref[pl.ds(q * n_in, n_in), h * half_rows : (h + 1) * half_rows],
                got,
                preferred_element_type=jnp.float32,
            ).astype(jnp.bfloat16)
            if h == 1:
                part = part + left[0:n_in, pl.ds(q * WIDE, WIDE)]
            left[0:n_in, pl.ds(q * WIDE, WIDE)] = part
            if h == 1:
                other = (q + 1) if q % 2 == 0 else (q - 1)
                left[n_in : 2 * n_in, pl.ds(other * WIDE, WIDE)] = -part if q % 2 == 0 else part
    vis = lax.dot_general(
        left[...], left[0:n_in, :], (((1,), (1,)), ((), ())), preferred_element_type=jnp.float32
    )
    vis = vis * (1.0 / math.sqrt(FRAMES * n_groups * A_LEN))
    rows = n_in // n_groups
    for k in range(n_groups):
        vpart[k, 0:rows] = vis[k * rows : (k + 1) * rows]
        vpart[k, rows : 2 * rows] = vis[n_in + k * rows : n_in + (k + 1) * rows]

    moves = []
    for dt in range(n_tile - 1, -1, -1):
        for dp in range(n_pol - 1, -1, -1):
            if dt or dp:
                pt, pp = (t + dt) % n_tile, (p + dp) % n_pol
                d = len(moves)
                move = pltpu.make_async_remote_copy(
                    src_ref=vpart.at[pt * n_pol + pp],
                    dst_ref=vrecv.at[d],
                    send_sem=vsend_sem.at[d],
                    recv_sem=vrecv_sem.at[d],
                    device_id={"tile": pt, "pol": pp},
                    device_id_type=MESH,
                )
                move.start()
                moves.append(move)
    total = vpart[g]
    for d, move in enumerate(moves):
        move.wait()
        total = total + vrecv[d]
    out_ref[0, 0] = total[:rows]
    out_ref[1, 0] = total[rows:]


def on_device_kernel(n_chan, n_tile, n_pol, voltages, flagged, channel_table):
    n_groups = n_tile * n_pol
    n_src = n_groups * n_chan
    n_in = n_src * IN_DEV
    consts = [jnp.asarray(x) for x in tables(n_groups, n_chan)]
    vmem = pl.BlockSpec(memory_space=pltpu.VMEM)
    operands = [voltages, flagged, channel_table, *consts]
    spaces = [pltpu.VMEM, pltpu.SMEM, pltpu.SMEM] + [pltpu.VMEM] * len(consts)
    rows = n_in // n_groups
    tiles = -(-voltages.shape[2] // LANES)
    tall = max(tiles, N_OUTER * N_INNER // LANES + A_PAD)
    return pl.pallas_call(
        functools.partial(kernel, n_chan, n_tile, n_pol),
        out_shape=jax.ShapeDtypeStruct((2, 1, rows, n_in), jnp.float32),
        in_specs=[pl.BlockSpec(memory_space=pl.ANY)] * len(operands),
        out_specs=vmem,
        scratch_shapes=[space(x.shape, x.dtype) for space, x in zip(spaces, operands)]
        + [
            pltpu.VMEM((tall * IN_DEV, LANES), jnp.float32),
            pltpu.VMEM((2, A_PAD, HALF_IN * FRAMES * LANES), jnp.bfloat16),
            pltpu.VMEM((2, WIDE, 2 * LANES), jnp.bfloat16),
            pltpu.VMEM((WIDE // LANES, R_ALL * ROWS, LANES), jnp.float32),
            pltpu.VMEM((2, R_ALL, ROWS, WIDE), jnp.bfloat16),
            pltpu.VMEM((2, n_src, ROWS, WIDE), jnp.bfloat16),
            pltpu.VMEM((2 * n_in, 4 * WIDE), jnp.bfloat16),
            pltpu.VMEM((n_groups, 2 * rows, n_in), jnp.float32),
            pltpu.VMEM((n_groups - 1, 2 * rows, n_in), jnp.float32),
            pltpu.SemaphoreType.DMA((len(operands),)),
            pltpu.SemaphoreType.DMA((2, n_src - 1)),
            pltpu.SemaphoreType.DMA((2, n_src - 1)),
            pltpu.SemaphoreType.DMA((n_groups - 1,)),
            pltpu.SemaphoreType.DMA((n_groups - 1,)),
        ],
        compiler_params=pltpu.CompilerParams(
            collective_id=0, has_side_effects=True, vmem_limit_bytes=60 * 1024 * 1024
        ),
    )(*operands)


def solution(mesh):
    n_chan, n_tile, n_pol = mesh.shape["chan"], mesh.shape["tile"], mesh.shape["pol"]
    body = on_device
    if n_chan * n_tile * n_pol == R_ALL:
        body = functools.partial(on_device_kernel, n_chan, n_tile, n_pol)
    in_specs = (P(("beam", "tile", "pol"), "chan", None), P(("tile", "pol"), "chan"), P())
    out_specs = P(None, ("beam", "chan"), ("tile", "pol"), None)
    return jax.shard_map(
        body, mesh=mesh, in_specs=in_specs, out_specs=out_specs, check_vma=False
    )
```

```python
import functools
import math

import jax
import jax.numpy as jnp
import numpy as np
from jax import lax
from jax.experimental import pallas as pl
from jax.experimental.pallas import tpu as pltpu
from jax.sharding import PartitionSpec as P

N_OUTER = 160
N_INNER = 125
TAPS = 4
FRAMES = 2


def window_table(tap_count, frame_len):
    position = np.arange(tap_count * frame_len) * 1.0
    centre = (position - tap_count * frame_len / 2.0 + 0.5) / frame_len
    shaped = np.sin(np.pi * centre) / (np.pi * centre)
    prototype = shaped * (
        0.5 - 0.5 * np.cos(2.0 * np.pi * (position + 0.5) / (tap_count * frame_len))
    )
    prototype = prototype / np.sqrt(np.sum(prototype * prototype) / frame_len)
    return prototype.reshape(tap_count, frame_len)


def make_spectra(samples_in, flags_in, channel_table, n_chan):
    in_dev = samples_in.shape[0]
    frame_len = N_OUTER * N_INNER
    half_len = N_OUTER // 2
    filt = jnp.asarray(window_table(TAPS, frame_len), jnp.float32)
    frames_all = samples_in.astype(jnp.float32).reshape(in_dev, FRAMES + TAPS - 1, frame_len)
    filtered = jnp.zeros((in_dev, FRAMES, frame_len), jnp.float32)
    for tap_index in range(TAPS):
        filtered = filtered + filt[tap_index] * frames_all[:, tap_index : tap_index + FRAMES]
    filtered = filtered.reshape(in_dev, FRAMES, N_INNER, N_OUTER)
    inner_idx = jnp.arange(N_INNER, dtype=jnp.int32)
    inner_ang = (
        2.0
        * math.pi
        / N_INNER
        * (inner_idx[:, None] * inner_idx[None, :] % N_INNER).astype(jnp.float32)
    )
    inner_mat = jnp.concatenate([jnp.cos(inner_ang), -jnp.sin(inner_ang)], axis=0)
    section_one = jnp.einsum("kn,vsnm->vskm", inner_mat, filtered, precision=lax.Precision.HIGH)
    real_one = section_one[:, :, :N_INNER]
    imag_one = section_one[:, :, N_INNER:]
    outer_idx = jnp.arange(N_OUTER, dtype=jnp.int32)
    twist_ang = (
        2.0
        * math.pi
        / frame_len
        * (inner_idx[:, None] * outer_idx[None, :] % frame_len).astype(jnp.float32)
    )
    twist_cos = jnp.cos(twist_ang)
    twist_sin = jnp.sin(twist_ang)
    real_two = real_one * twist_cos + imag_one * twist_sin
    imag_two = imag_one * twist_cos - real_one * twist_sin
    joined = jnp.concatenate([real_two, imag_two], axis=3)
    block_width = half_len // n_chan
    out_pos = jnp.arange(half_len, dtype=jnp.int32)
    owner = out_pos // block_width
    onehot = owner[:, None] == jnp.arange(n_chan, dtype=jnp.int32)[None, :]
    chosen = jnp.sum(jnp.where(onehot, channel_table[None, :], 0), axis=1)
    outer_k = chosen * block_width + out_pos % block_width
    outer_ang = (
        2.0
        * math.pi
        / N_OUTER
        * (outer_k[:, None] * outer_idx[None, :] % N_OUTER).astype(jnp.float32)
    )
    outer_cos = jnp.cos(outer_ang)
    outer_sin = jnp.sin(outer_ang)
    real_rows = jnp.concatenate([outer_cos, outer_sin], axis=1)
    imag_rows = jnp.concatenate([-outer_sin, outer_cos], axis=1)
    outer_mat = jnp.stack([real_rows, imag_rows], axis=0)
    spectrum = jnp.einsum("vskn,rjn->vrsjk", joined, outer_mat, precision=lax.Precision.HIGH)
    spectrum = spectrum.reshape(in_dev, 2, FRAMES, half_len * N_INNER)
    kept_mask = (1 - flags_in).astype(jnp.float32)
    spectrum = spectrum * (kept_mask[:, None, None, None] / math.sqrt(frame_len))
    return spectrum.astype(jnp.bfloat16)


def correlate(left_rows, panel_cols, scale):
    return (
        jnp.einsum("rik,jk->rij", left_rows, panel_cols, preferred_element_type=jnp.float32) * scale
    )


def on_device(voltages, flagged, channel_table):
    n_chan = lax.axis_size("chan")
    spectra = make_spectra(voltages[0], flagged[0], channel_table, n_chan)
    turned = lax.all_to_all(spectra, "chan", split_axis=3, concat_axis=0, tiled=True)
    group_len = turned.shape[0]
    chb_len = turned.shape[3]
    half_k = FRAMES * chb_len
    scale = 1.0 / math.sqrt(FRAMES * chb_len)
    band_rows = turned.reshape(group_len, 2 * half_k)
    swapped = jnp.concatenate([band_rows[:, half_k:], -band_rows[:, :half_k]], axis=1)
    left_rows = jnp.stack([band_rows, swapped], axis=0)
    vis_local = correlate(
        left_rows, lax.all_gather(band_rows, ("tile", "pol"), axis=0, tiled=True), scale
    )
    return vis_local[:, None]


MESH = pl.DeviceIdType.MESH
LANES = 128
A_LEN = 625
A_PAD = 640
K0_HALF = 313
K0_PAD = 320
R_ALL = 16
IN_DEV = 8
PITCH = 9
SPLIT = 2
HALF_IN = 4
ROWS = 16
WIDE = FRAMES * K0_PAD


def split_bf16(table):
    high = table.astype(jnp.bfloat16)
    low = (table - high.astype(np.float64)).astype(jnp.bfloat16)
    return high, low


def tables(n_groups, n_chan):
    frame_len = N_OUTER * N_INNER
    window = window_table(TAPS, frame_len).reshape(-1).astype(np.float32).astype(np.float64)
    shift = frame_len // LANES
    win = np.zeros((FRAMES, A_PAD * LANES))
    win[0, : window.size] = window
    offset = frame_len - shift * LANES
    win[1, offset : offset + window.size] = window
    win = win.reshape(FRAMES, A_PAD, LANES)

    k0 = np.arange(K0_HALF)
    a = np.arange(A_LEN + 1)
    ang = 2.0 * np.pi / A_LEN * ((4 * k0[:, None] * a[None, :]) % A_LEN)
    dft = np.zeros((2, K0_PAD, A_PAD))
    dft[0, :K0_HALF, : A_LEN + 1] = np.cos(ang)
    dft[1, :K0_HALF, : A_LEN + 1] = -np.sin(ang)
    dft = dft.reshape(2 * K0_PAD, A_PAD)

    b = np.arange(LANES)
    twist = np.zeros((FRAMES, 2, K0_PAD, LANES))
    for s in range(FRAMES):
        first = s * shift * LANES
        ang = 2.0 * np.pi / frame_len * ((k0[:, None] * (b[None, :] + first)) % frame_len)
        twist[s, 0, :K0_HALF] = np.cos(ang)
        twist[s, 1, :K0_HALF] = np.sin(ang)
    twist = twist / math.sqrt(frame_len)

    r = np.arange(R_ALL)
    ang = 2.0 * np.pi / 32 * ((r[:, None] * b[None, :]) % 32)
    mir = 2.0 * np.pi / 32 * (((31 - r)[:, None] * b[None, :]) % 32)
    outer = np.zeros((R_ALL, 4, 2, LANES))
    outer[:, 0, 0], outer[:, 0, 1] = np.cos(ang), np.sin(ang)
    outer[:, 1, 0], outer[:, 1, 1] = -np.sin(ang), np.cos(ang)
    outer[:, 2, 0], outer[:, 2, 1] = np.cos(mir), np.sin(mir)
    outer[:, 3, 0], outer[:, 3, 1] = np.sin(mir), -np.cos(mir)
    outer = outer.reshape(n_chan, n_groups * 4, 2 * LANES)
    outer = np.stack(split_bf16(outer), axis=1)

    n_src = n_groups * n_chan
    perm = np.zeros((4, n_src * IN_DEV, 2, n_src, 4, HALF_IN))
    for src in range(n_src):
        for h in range(2):
            for i in range(HALF_IN):
                for q in range(4):
                    perm[q, src * IN_DEV + h * HALF_IN + i, h, src, q, i] = 1.0
    size = 4 * n_src * IN_DEV
    perm = perm.reshape(size, size).astype(jnp.bfloat16)
    return win.astype(np.float32), dft.astype(jnp.bfloat16), twist.astype(np.float32), outer, perm


def kernel(
    n_chan, n_tile, n_pol, volt_hbm, flag_hbm, table_hbm, win_hbm, dh_hbm, twist_hbm,
    outer_hbm, perm_hbm, out_ref, volt_ref, flag_ref, table_ref, win_ref, dh_ref, twist_ref,
    outer_ref, perm_ref, flat, u_all, zt, turned, send, recv, left, vpart, vrecv,
    load_sem, send_sem, recv_sem, vsend_sem, vrecv_sem,
):
    loads = [
        pltpu.make_async_copy(source, target, load_sem.at[n])
        for n, (source, target) in enumerate(
            [
                (volt_hbm, volt_ref), (win_hbm, win_ref), (dh_hbm, dh_ref),
                (twist_hbm, twist_ref), (outer_hbm, outer_ref), (flag_hbm, flag_ref),
                (table_hbm, table_ref), (perm_hbm, perm_ref),
            ]
        )
    ]
    for load in loads:
        load.start()
    n_groups = n_tile * n_pol
    c, t, p = lax.axis_index("chan"), lax.axis_index("tile"), lax.axis_index("pol")
    g = t * n_pol + p
    src = g * n_chan + c

    def peers():
        found = []
        for dc in sorted(range(n_chan), key=lambda dc: (dc == 0, abs(2 * dc - n_chan))):
            for dt in range(n_tile - 1, -1, -1):
                for dp in range(n_pol - 1, -1, -1):
                    if dc or dt or dp:
                        found.append(((c + dc) % n_chan, (t + dt) % n_tile, (p + dp) % n_pol))
        return found

    def where(peer):
        return {"chan": peer[0], "tile": peer[1], "pol": peer[2]}

    everyone = peers()
    early = SPLIT * n_groups
    moves = [[], []]
    for d, peer in enumerate(everyone):
        slot = peer[0] * n_groups + peer[1] * n_pol + peer[2]
        for h in range(2):
            if d < early:
                source, target = send.at[slot, h], recv.at[src, h]
            elif h == 1:
                source, target = send.at[slot], recv.at[src]
            else:
                continue
            moves[h].append(
                pltpu.make_async_remote_copy(
                    src_ref=source,
                    dst_ref=target,
                    send_sem=send_sem.at[h, d],
                    recv_sem=recv_sem.at[h, d],
                    device_id=where(peer),
                    device_id_type=MESH,
                )
            )
    barrier = pltpu.get_barrier_semaphore()
    for peer in everyone:
        pl.semaphore_signal(barrier, inc=1, device_id=where(peer), device_id_type=MESH)

    tiles_full = volt_ref.shape[2] // LANES
    rest = volt_ref.shape[2] - tiles_full * LANES
    flat[pl.ds(tiles_full * PITCH, flat.shape[0] - tiles_full * PITCH), :] = jnp.zeros(
        (flat.shape[0] - tiles_full * PITCH, LANES), jnp.float32
    )
    step = 71
    loads[0].wait()
    if rest:
        flat[pl.ds(tiles_full * PITCH, IN_DEV), pl.ds(0, rest)] = volt_ref[
            0, :, pl.ds(tiles_full * LANES, rest)
        ].astype(jnp.float32)

    def spread(chunk, carry):
        for j in range(step):
            tile = chunk * step + j
            lane = pl.multiple_of(tile * LANES, LANES)
            row = tile * PITCH
            flat[pl.ds(row, IN_DEV), :] = volt_ref[0, :, pl.ds(lane, LANES)].astype(jnp.float32)
        return carry

    lax.fori_loop(0, tiles_full // step, spread, 0)

    for load in loads[1:7]:
        load.wait()
    outer_rows = jnp.concatenate(
        [outer_ref[table_ref[b], part] for part in range(2) for b in range(n_chan)], axis=0
    )
    shift = N_OUTER * N_INNER // LANES
    n_rows = R_ALL * 4
    row_id = lax.broadcasted_iota(jnp.int32, (n_rows, WIDE), 0)
    lane_id = lax.broadcasted_iota(jnp.int32, (n_rows, WIDE), 1)
    twice = ((row_id % 4) >= 2) & ((lane_id == 0) | (lane_id == K0_PAD))
    once = jnp.where(twice, 0.0, 1.0)

    for h in range(2):
        for i in range(HALF_IN):
            for s in range(FRAMES):
                first = s * shift * PITCH + h * HALF_IN + i
                col = (i * FRAMES + s) * LANES
                u = flat[pl.ds(first, A_PAD, stride=PITCH), :] * win_ref[s]
                u_all[h, :, col : col + LANES] = u.astype(jnp.bfloat16)
        for i in range(HALF_IN):
            for s in range(FRAMES):
                col = (i * FRAMES + s) * LANES
                if s == 0:
                    wide = pl.ds(i * FRAMES * LANES, FRAMES * LANES)
                    y = jnp.dot(dh_ref[...], u_all[h, :, wide], preferred_element_type=jnp.float32)
                yr = y[:K0_PAD, s * LANES : (s + 1) * LANES]
                yi = y[K0_PAD:, s * LANES : (s + 1) * LANES]
                co, si = twist_ref[s, 0], twist_ref[s, 1]
                zt[i % 2, pl.ds(s * K0_PAD, K0_PAD), 0:LANES] = (yr * co + yi * si).astype(jnp.bfloat16)
                zt[i % 2, pl.ds(s * K0_PAD, K0_PAD), LANES : 2 * LANES] = (yi * co - yr * si).astype(
                    jnp.bfloat16
                )
            x = lax.dot_general(
                outer_rows, zt[i % 2], (((1,), (1,)), ((), ())), preferred_element_type=jnp.float32
            )
            keep = (1 - flag_ref[0, h * HALF_IN + i]).astype(jnp.float32)
            x = (x[:n_rows] + x[n_rows:]) * (once * keep)
            for l in range(WIDE // LANES):
                turned[l, pl.ds(i, n_rows, stride=HALF_IN), :] = x[:, l * LANES : (l + 1) * LANES]
        for l in range(WIDE // LANES):
            send[:, h, :, pl.ds(l * LANES, LANES)] = (
                turned[l].astype(jnp.bfloat16).reshape(R_ALL, ROWS, LANES)
            )
        if h == 0:
            pl.semaphore_wait(barrier, len(everyone))
        for move in moves[h]:
            move.start()
        recv[src, h] = send[c * n_groups + g, h]

    loads[7].wait()
    n_in = n_groups * n_chan * IN_DEV
    half_rows = n_groups * n_chan * ROWS
    for move in moves[0] + moves[1]:
        move.wait()
    for h in range(2):
        got = recv[:, h].reshape(half_rows, WIDE)
        for q in range(4):
            part = jnp.dot(
                perm_ref[pl.ds(q * n_in, n_in), h * half_rows : (h + 1) * half_rows],
                got,
                preferred_element_type=jnp.float32,
            ).astype(jnp.bfloat16)
            if h == 1:
                part = part + left[0:n_in, pl.ds(q * WIDE, WIDE)]
            left[0:n_in, pl.ds(q * WIDE, WIDE)] = part
            if h == 1:
                other = (q + 1) if q % 2 == 0 else (q - 1)
                left[n_in : 2 * n_in, pl.ds(other * WIDE, WIDE)] = -part if q % 2 == 0 else part
    vis = lax.dot_general(
        left[...], left[0:n_in, :], (((1,), (1,)), ((), ())), preferred_element_type=jnp.float32
    )
    vis = vis * (1.0 / math.sqrt(FRAMES * n_groups * A_LEN))
    rows = n_in // n_groups
    for k in range(n_groups):
        vpart[k, 0:rows] = vis[k * rows : (k + 1) * rows]
        vpart[k, rows : 2 * rows] = vis[n_in + k * rows : n_in + (k + 1) * rows]

    moves = []
    for dt in range(n_tile - 1, -1, -1):
        for dp in range(n_pol - 1, -1, -1):
            if dt or dp:
                pt, pp = (t + dt) % n_tile, (p + dp) % n_pol
                d = len(moves)
                move = pltpu.make_async_remote_copy(
                    src_ref=vpart.at[pt * n_pol + pp],
                    dst_ref=vrecv.at[d],
                    send_sem=vsend_sem.at[d],
                    recv_sem=vrecv_sem.at[d],
                    device_id={"tile": pt, "pol": pp},
                    device_id_type=MESH,
                )
                move.start()
                moves.append(move)
    total = vpart[g]
    for d, move in enumerate(moves):
        move.wait()
        total = total + vrecv[d]
    out_ref[0, 0] = total[:rows]
    out_ref[1, 0] = total[rows:]


def on_device_kernel(n_chan, n_tile, n_pol, voltages, flagged, channel_table):
    n_groups = n_tile * n_pol
    n_src = n_groups * n_chan
    n_in = n_src * IN_DEV
    consts = [jnp.asarray(x) for x in tables(n_groups, n_chan)]
    vmem = pl.BlockSpec(memory_space=pltpu.VMEM)
    operands = [voltages, flagged, channel_table, *consts]
    spaces = [pltpu.VMEM, pltpu.SMEM, pltpu.SMEM] + [pltpu.VMEM] * len(consts)
    rows = n_in // n_groups
    tiles = -(-voltages.shape[2] // LANES)
    tall = max(tiles, N_OUTER * N_INNER // LANES + A_PAD)
    return pl.pallas_call(
        functools.partial(kernel, n_chan, n_tile, n_pol),
        out_shape=jax.ShapeDtypeStruct((2, 1, rows, n_in), jnp.float32),
        in_specs=[pl.BlockSpec(memory_space=pl.ANY)] * len(operands),
        out_specs=vmem,
        scratch_shapes=[space(x.shape, x.dtype) for space, x in zip(spaces, operands)]
        + [
            pltpu.VMEM((tall * PITCH, LANES), jnp.float32),
            pltpu.VMEM((2, A_PAD, HALF_IN * FRAMES * LANES), jnp.bfloat16),
            pltpu.VMEM((2, WIDE, 2 * LANES), jnp.bfloat16),
            pltpu.VMEM((WIDE // LANES, R_ALL * ROWS, LANES), jnp.float32),
            pltpu.VMEM((R_ALL, 2, ROWS, WIDE), jnp.bfloat16),
            pltpu.VMEM((n_src, 2, ROWS, WIDE), jnp.bfloat16),
            pltpu.VMEM((2 * n_in, 4 * WIDE), jnp.bfloat16),
            pltpu.VMEM((n_groups, 2 * rows, n_in), jnp.float32),
            pltpu.VMEM((n_groups - 1, 2 * rows, n_in), jnp.float32),
            pltpu.SemaphoreType.DMA((len(operands),)),
            pltpu.SemaphoreType.DMA((2, n_src - 1)),
            pltpu.SemaphoreType.DMA((2, n_src - 1)),
            pltpu.SemaphoreType.DMA((n_groups - 1,)),
            pltpu.SemaphoreType.DMA((n_groups - 1,)),
        ],
        compiler_params=pltpu.CompilerParams(
            collective_id=0, has_side_effects=True, vmem_limit_bytes=60 * 1024 * 1024
        ),
    )(*operands)


def solution(mesh):
    n_chan, n_tile, n_pol = mesh.shape["chan"], mesh.shape["tile"], mesh.shape["pol"]
    body = on_device
    if n_chan * n_tile * n_pol == R_ALL:
        body = functools.partial(on_device_kernel, n_chan, n_tile, n_pol)
    in_specs = (P(("beam", "tile", "pol"), "chan", None), P(("tile", "pol"), "chan"), P())
    out_specs = P(None, ("beam", "chan"), ("tile", "pol"), None)
    return jax.shard_map(
        body, mesh=mesh, in_specs=in_specs, out_specs=out_specs, check_vma=False
    )
```
